256 devices in a mesh: seq: 16 (over z, x_lo), col: 16 (over x_hi, y, core).
Axes of the slice: x: 4 (x_hi: 2, x_lo: 2; x = x_hi * 2 + x_lo), y: 4, z: 8, core: 2. Of those that a mesh axis runs over, the one named last changes fastest.
Arguments:
- tokens: bfloat16 [2048, 4096], P('seq'), may hold values from -6 to 6
- gate_weight: bfloat16 [8, 4096, 11008], P(None, 'seq', 'col'), may hold values from -0.25 to 0.25
- up_weight: bfloat16 [8, 4096, 11008], P(None, 'seq', 'col'), may hold values from -0.25 to 0.25
- down_weight: bfloat16 [8, 11008, 4096], P(None, 'col', 'seq'), may hold values from -0.15625 to 0.15625
- cotangent: bfloat16 [2048, 4096], P(None, 'seq'), may hold values from -6 to 6
- route: int32 [8, 8], replicated, may hold values from 16 to 255
- doc_start: int32 [8], replicated, may hold values 0 or 1
Outputs:
- mixed: bfloat16 [2048, 4096], P('col', 'seq')
- grad_tokens: bfloat16 [2048, 4096], P('col', 'seq')
- grad_route: float32 [8, 8], replicated
The draws below stay inside these ranges and needn't reach their ends.
All inputs are finite; a program needn't handle non-finite values.
Results may differ from the reference program's by a relative error of at most 0.0073.
Values may be sent and summed in bfloat16 or wider, within the bound.
No kernel may reach another device: no remote copies, remote signals or barrier semaphores. Data moves between devices by JAX's collectives and lax.ppermute only.
A program may use at most 128 MiB of HBM per device.

```python
import jax
import jax.numpy as jnp
from jax import lax

D = 4096
FF = 11008
E = 8
TOKENS = 2048
SEGS = 8


def place_ends(result, key, low, top_value):
    index_at = [jax.random.randint(jax.random.fold_in(key, axis), (), 0, length) for axis, length in enumerate(result.shape)]
    main_axis = result.shape.index(max(result.shape))
    beside = index_at[:main_axis] + [(index_at[main_axis] + 1) % result.shape[main_axis]] + index_at[main_axis + 1:]
    return result.at[tuple(index_at)].set(low).at[tuple(beside)].set(top_value)


def block_levels(key, dims, shards, least, largest):
    def one(position, parts):
        heights = jax.random.uniform(jax.random.fold_in(jax.random.fold_in(key, 6), position), (parts,), jnp.float32, least / len(shards), largest / len(shards))
        return jnp.repeat(jnp.exp(heights), dims[position] // parts).reshape((-1,) + (1,) * (len(dims) - position - 1))

    factor_of = one(*shards[0])
    for cut in shards[1:]:
        factor_of = factor_of * one(*cut)
    return factor_of


def normal_values(rng, extent, spread, limit, cuts=(), held_as=jnp.bfloat16):
    factor_of = block_levels(rng, extent, cuts, -0.22, 0.18) if cuts else 1.0
    values = jax.random.normal(rng, extent, jnp.float32) * spread * factor_of
    return jnp.minimum(jnp.maximum(values, -limit), limit).astype(held_as)


def setup_inputs(seed: int = 0) -> dict:
    splits = jax.random.split(jax.random.key(seed), 8)
    tokens = normal_values(splits[0], (TOKENS, D), 1.0, 6.0, ((0, 16),))
    gate_weight = normal_values(splits[1], (E, D, FF), (D // 8) ** -0.5, 0.25, ((1, 16), (2, 16)))
    up_weight = normal_values(splits[2], (E, D, FF), (D // 8) ** -0.5, 0.25, ((1, 16), (2, 16)))
    down_weight = normal_values(splits[3], (E, FF, D), (FF // 8) ** -0.5, 0.15625, ((1, 16), (2, 16)))
    cotangent = normal_values(splits[4], (TOKENS, D), 1.0, 6.0, ((1, 16),))
    route = place_ends(jax.random.randint(splits[5], (SEGS, E), 16, 256), jax.random.fold_in(splits[5], 1), 16, 255).astype(jnp.int32)
    doc_start = place_ends((jax.random.randint(splits[6], (SEGS,), 0, 3) < 1).astype(jnp.int32), jax.random.fold_in(splits[6], 1), 0, 1)
    return dict(tokens=tokens, gate_weight=gate_weight, up_weight=up_weight, down_weight=down_weight, cotangent=cotangent, route=route, doc_start=doc_start)


def routing(route, doc_start):
    own = route.astype(jnp.float32) / 1024.0
    prev = jnp.concatenate([own[:1], own[:-1]], axis=0)
    first = jnp.arange(route.shape[0]) == 0
    keep = jnp.logical_or(first, doc_start == 1)
    return jnp.where(keep[:, None], own, prev), keep


def route_gradient(merge_grad, keep):
    own_part = jnp.where(keep[:, None], merge_grad, jnp.float32(0.0))
    next_part = jnp.where(keep[:, None], jnp.float32(0.0), merge_grad)
    next_part = jnp.concatenate([next_part[1:], jnp.zeros_like(next_part[:1])], axis=0)
    return (own_part + next_part) / 1024.0


def blend(weights, table_row):
    total = table_row[0] * weights[0].astype(jnp.float32)
    for expert in range(1, weights.shape[0]):
        total = total + table_row[expert] * weights[expert].astype(jnp.float32)
    return total.astype(jnp.bfloat16)


def reference(tokens, gate_weight, up_weight, down_weight, cotangent, route, doc_start):
    used, keep = routing(route, doc_start)
    width = tokens.shape[1]

    def one_segment(items):
        rows, grads, table_row = items
        w_gate = blend(gate_weight, table_row)
        w_up = blend(up_weight, table_row)
        w_down = blend(down_weight, table_row)
        gate = jnp.dot(rows, w_gate, preferred_element_type=jnp.float32)
        up = jnp.dot(rows, w_up, preferred_element_type=jnp.float32)
        sig = jax.nn.sigmoid(gate)
        act = (gate * sig * up).astype(jnp.bfloat16)
        out = jnp.dot(act, w_down, preferred_element_type=jnp.float32).astype(jnp.bfloat16)
        grad_act = jnp.dot(grads, w_down.T, preferred_element_type=jnp.float32)
        grad_gate = (grad_act * up * sig * (1.0 + gate * (1.0 - sig))).astype(jnp.bfloat16)
        grad_up = (grad_act * gate * sig).astype(jnp.bfloat16)
        grad_rows = (jnp.dot(grad_gate, w_gate.T, preferred_element_type=jnp.float32)
                     + jnp.dot(grad_up, w_up.T, preferred_element_type=jnp.float32)).astype(jnp.bfloat16)
        outer_gate = jnp.dot(rows.T, grad_gate, preferred_element_type=jnp.float32).astype(jnp.bfloat16).astype(jnp.float32)
        outer_up = jnp.dot(rows.T, grad_up, preferred_element_type=jnp.float32).astype(jnp.bfloat16).astype(jnp.float32)
        outer_down = jnp.dot(act.T, grads, preferred_element_type=jnp.float32).astype(jnp.bfloat16).astype(jnp.float32)
        terms = []
        for expert in range(gate_weight.shape[0]):
            value = jnp.sum(outer_gate * gate_weight[expert].astype(jnp.float32))
            value = value + jnp.sum(outer_up * up_weight[expert].astype(jnp.float32))
            value = value + jnp.sum(outer_down * down_weight[expert].astype(jnp.float32))
            terms.append(value)
        return out, grad_rows, jnp.stack(terms)

    segs = route.shape[0]
    seg_len = tokens.shape[0] // segs
    mixed, grad_tokens, merge_grad = lax.map(
        one_segment,
        (tokens.reshape(segs, seg_len, width), cotangent.reshape(segs, seg_len, width), used))
    grad_route = route_gradient(merge_grad, keep)
    return mixed.reshape(-1, width), grad_tokens.reshape(-1, width), grad_route
```

```python
import jax
import jax.numpy as jnp
from jax import lax
from jax.experimental import pallas as pl
from jax.experimental.pallas import tpu as pltpu
from jax.sharding import Mesh, PartitionSpec as P

SEQ = ("z", "xl")
COL = ("xh", "y", "core")
NZ = 8
TILE = 16
BF = jnp.bfloat16
F32 = jnp.float32
VMEM_BYTES = 56 * 1024 * 1024


def routing(route, doc_start):
    own = route.astype(F32) / 1024.0
    prev = jnp.concatenate([own[:1], own[:-1]], axis=0)
    first = jnp.arange(route.shape[0]) == 0
    keep = jnp.logical_or(first, doc_start == 1)
    return jnp.where(keep[:, None], own, prev), keep


def route_gradient(merge_grad, keep):
    own_part = jnp.where(keep[:, None], merge_grad, jnp.float32(0.0))
    next_part = jnp.where(keep[:, None], jnp.float32(0.0), merge_grad)
    next_part = jnp.concatenate([next_part[1:], jnp.zeros_like(next_part[:1])], axis=0)
    return (own_part + next_part) / 1024.0


def dot(a, b, ca, cb):
    return lax.dot_general(a, b, (((ca,), (cb,)), ((), ())), preferred_element_type=F32)


def params():
    return pltpu.CompilerParams(vmem_limit_bytes=VMEM_BYTES)


def cost(flops, nbytes):
    return pl.CostEstimate(flops=flops, bytes_accessed=nbytes, transcendentals=0)


def merge_kernel(n, *refs):
    table = refs[0][...]
    experts, rows, width = refs[1].shape

    def step(j, carry):
        at = pl.ds(pl.multiple_of(j * TILE, TILE), TILE)
        for w, out in zip(refs[1 : 1 + n], refs[1 + n :]):
            tile = w[:, at, :].reshape(experts * TILE, width)
            out[:, at, :] = dot(table, tile, 1, 0).astype(BF).reshape(experts, TILE, width)
        return carry

    lax.fori_loop(0, rows // TILE, step, 0)


def merge(table, *weights):
    n = len(weights)
    size = weights[0].size
    return pl.pallas_call(
        lambda *refs: merge_kernel(n, *refs),
        out_shape=[jax.ShapeDtypeStruct(w.shape, BF) for w in weights],
        compiler_params=params(),
        cost_estimate=cost(2 * 128 * n * size, 4 * n * size),
        name="merge",
    )(table, *weights)


def at_segment(k):
    return lambda i, s: (lax.rem(s[0] + k, NZ), 0, 0)


def at_own(k):
    return lambda i, s: (2 * lax.rem(s[0] + k, NZ) + s[1], 0, 0)


def at_other(k):
    return lambda i, s: (2 * lax.rem(s[0] + k, NZ) + 1 - s[1], 0, 0)


def whole(shape):
    return pl.BlockSpec(shape, lambda i, s: (0,) * len(shape))


def partial_products(where, ks, mats, blocks, split):
    rows, width = mats[0].shape[1:]
    tok = blocks.shape[1]
    n = len(mats)
    per = n + 2
    specs = []
    args = []
    for k in ks:
        specs += [pl.BlockSpec((1, rows, width), at_segment(k))] * n
        specs += [pl.BlockSpec((1, tok, width), at_own(k)), pl.BlockSpec((1, tok, width), at_other(k))]
        args += list(mats) + [blocks, blocks]
    if split:
        shapes = [jax.ShapeDtypeStruct((n * rows, tok), BF)] * len(ks)
        shapes.append(jax.ShapeDtypeStruct((len(ks), n * rows, tok), BF))
    else:
        shapes = [jax.ShapeDtypeStruct((n * rows, 2 * tok), BF)] * len(ks)

    def kernel(s_ref, *refs):
        outs = refs[per * len(ks) :]
        for i in range(len(ks)):
            part = refs[per * i : per * (i + 1)]
            both = jnp.concatenate([part[n][0], part[n + 1][0]], axis=0)
            for m in range(n):
                r = dot(part[m][0], both, 1, 1).astype(BF)
                if split:
                    outs[i][m * rows : (m + 1) * rows, :] = r[:, :tok]
                    outs[-1][i, m * rows : (m + 1) * rows, :] = r[:, tok:]
                else:
                    outs[i][m * rows : (m + 1) * rows, :] = r

    return pl.pallas_call(
        kernel,
        grid_spec=pltpu.PrefetchScalarGridSpec(
            num_scalar_prefetch=1,
            grid=(1,),
            in_specs=specs,
            out_specs=[whole(s.shape) for s in shapes],
        ),
        out_shape=shapes,
        compiler_params=params(),
        cost_estimate=cost(4 * len(ks) * n * rows * width * tok, 4 * len(ks) * n * rows * width),
        name="products",
    )(where, *args)


def segment_backward(where, k, act, own, other, tok_blocks, cot_blocks, m_gate, m_up, m_down, sums):
    rows, width = m_gate.shape[1:]
    tok = tok_blocks.shape[1]
    segs = m_gate.shape[0]

    def kernel(s_ref, act_r, own_r, oth_r, to_r, tp_r, co_r, cp_r, g_r, u_r, d_r, *rest):
        out, o_gate, o_up, o_down = rest[-4:]
        a = act_r[...]
        gg = jnp.concatenate([own_r[:rows, :], oth_r[:rows, :]], axis=1)
        gu = jnp.concatenate([own_r[rows:, :], oth_r[rows:, :]], axis=1)
        tokens = jnp.concatenate([to_r[0], tp_r[0]], axis=0)
        cots = jnp.concatenate([co_r[0], cp_r[0]], axis=0)
        mixed = dot(a, d_r[0], 0, 0).astype(BF)
        back = (dot(gg, g_r[0], 0, 0) + dot(gu, u_r[0], 0, 0)).astype(BF)
        mine = s_ref[1]
        out[0, mine, :, :width] = mixed[:tok]
        out[0, mine, :, width:] = back[:tok]
        out[0, 1 - mine, :, :width] = mixed[tok:]
        out[0, 1 - mine, :, width:] = back[tok:]
        o_gate[0] = dot(gg, tokens, 1, 0).astype(BF)
        o_up[0] = dot(gu, tokens, 1, 0).astype(BF)
        o_down[0] = dot(a, cots, 1, 0).astype(BF)

    shapes = [jax.ShapeDtypeStruct((segs, 2, tok, 2 * width), BF)]
    shapes += [jax.ShapeDtypeStruct((segs, rows, width), BF)] * 3
    seg = pl.BlockSpec((1, rows, width), at_segment(k))
    specs = [
        whole(act.shape),
        whole(own.shape),
        whole(other.shape),
        pl.BlockSpec((1, tok, width), at_own(k)),
        pl.BlockSpec((1, tok, width), at_other(k)),
        pl.BlockSpec((1, tok, width), at_own(k)),
        pl.BlockSpec((1, tok, width), at_other(k)),
        seg,
        seg,
        seg,
    ]
    args = [act, own, other, tok_blocks, tok_blocks, cot_blocks, cot_blocks, m_gate, m_up, m_down]
    aliases = {}
    if sums is not None:
        aliases = {1 + len(args) + i: i for i in range(4)}
        specs += [pl.BlockSpec(memory_space=pl.ANY)] * 4
        args += list(sums)
    return pl.pallas_call(
        kernel,
        grid_spec=pltpu.PrefetchScalarGridSpec(
            num_scalar_prefetch=1,
            grid=(1,),
            in_specs=specs,
            out_specs=[
                pl.BlockSpec((1, 2, tok, 2 * width), lambda i, s: (lax.rem(s[0] + k, NZ), 0, 0, 0)),
                seg,
                seg,
                seg,
            ],
        ),
        out_shape=shapes,
        input_output_aliases=aliases,
        compiler_params=params(),
        cost_estimate=cost(24 * rows * width * tok, 20 * rows * width),
        name="backward",
    )(where, *args)


def route_kernel(*refs):
    out = refs[6]
    segs, rows, width = refs[0].shape
    out[...] = jnp.zeros_like(out)

    def step(j, carry):
        at = pl.ds(pl.multiple_of(j * TILE, TILE), TILE)
        total = out[...]
        for o, w in zip(refs[:3], refs[3:6]):
            total += dot(
                o[:, at, :].reshape(segs * TILE, width), w[:, at, :].reshape(segs * TILE, width), 1, 1
            )
        out[...] = total
        return carry

    lax.fori_loop(0, rows // TILE, step, 0)


def route_products(outers, weights):
    segs = outers[0].shape[0]
    size = outers[0].size
    full = pl.pallas_call(
        route_kernel,
        out_shape=jax.ShapeDtypeStruct((segs * TILE, segs * TILE), F32),
        compiler_params=params(),
        cost_estimate=cost(6 * 128 * size, 12 * size),
        name="route_products",
    )(*outers, *weights)
    picked = full.reshape(segs, TILE, segs, TILE) * jnp.eye(TILE, dtype=F32)[None, :, None, :]
    return jnp.sum(picked, axis=(1, 3))


def shift(x, axis, n, by):
    return lax.ppermute(x, axis, [(i, (i + by) % n) for i in range(n)])


def swap(x, axis):
    return shift(x, axis, 2, 1)


def add(a, b):
    return a.astype(F32) + b.astype(F32)


def ring_sum(blocks):
    up, down = blocks[4].astype(BF), blocks[5].astype(BF)
    up, down = shift(up, "z", NZ, 1), shift(down, "z", NZ, -1)
    up, down = add(up, blocks[3]).astype(BF), add(down, blocks[6]).astype(BF)
    up, down = shift(up, "z", NZ, 1), shift(down, "z", NZ, -1)
    up, down = add(up, blocks[2]).astype(BF), add(down, blocks[7]).astype(BF)
    up, down = shift(up, "z", NZ, 1), shift(down, "z", NZ, -1)
    up = add(up, blocks[1]).astype(BF)
    up = shift(up, "z", NZ, 1)
    return add(up, down) + blocks[0]


def ring_gather(block):
    found = {0: block}
    up = down = block
    for step in range(1, 4):
        up, down = shift(up, "z", NZ, 1), shift(down, "z", NZ, -1)
        found[NZ - step], found[step] = up, down
    found[4] = shift(down, "z", NZ, -1)
    return [found[k] for k in range(NZ)]


def total_over_all(x):
    for axis in ("core", "xl", "xh"):
        x = x + swap(x, axis)
    for axis, n in (("y", 4), ("z", NZ)):
        far = 1
        while far < n:
            x = x + lax.ppermute(x, axis, [(i, i ^ far) for i in range(n)])
            far *= 2
    return x


def on_device(tokens, gate_weight, up_weight, down_weight, cotangent, route, doc_start):
    tok, width_all = tokens.shape
    experts, width, cols = gate_weight.shape
    segs = route.shape[0]
    n_seq = 2 * NZ
    where = jnp.stack([lax.axis_index("z"), lax.axis_index("xl")]).astype(jnp.int32)
    used, keep = routing(route, doc_start)
    table = used.astype(BF)[:, None, :, None] * jnp.eye(TILE, dtype=BF)[None, :, None, :]
    table = table.reshape(segs * TILE, experts * TILE)

    tok_blocks = lax.all_to_all(
        tokens.reshape(tok, n_seq, width).swapaxes(0, 1), SEQ, split_axis=0, concat_axis=0, tiled=True
    )
    cot_blocks = cotangent.reshape(n_seq, tok, width)
    gate_weight = gate_weight.swapaxes(1, 2)
    up_weight = up_weight.swapaxes(1, 2)

    (m_down,) = merge(table, down_weight)
    m_gate, m_up = merge(table, gate_weight, up_weight)

    first = partial_products(where, (4, 5), (m_down,), cot_blocks, False)
    rest = partial_products(where, (3, 6, 2, 7, 1, 0), (m_down,), cot_blocks, False)
    parts = dict(zip((4, 5, 3, 6, 2, 7, 1, 0), list(first) + list(rest)))
    both = ring_sum([parts[k] for k in range(NZ)])
    grad_act = both[:, :tok] + swap(both[:, tok:].astype(BF), "xl").astype(F32)

    parts = {}
    for ks in ((4, 5), (3, 6), (2, 7), (1,), (0,)):
        *kept, sent = partial_products(where, ks, (m_gate, m_up), tok_blocks, True)
        came = swap(sent, "xl")
        for i, k in enumerate(ks):
            parts[k] = add(kept[i], came[i])
    pre = ring_sum([parts[k] for k in range(NZ)])

    gate, up = pre[:cols], pre[cols:]
    sig = jax.nn.sigmoid(gate)
    act = (gate * sig * up).astype(BF)
    grad_gate = grad_act * up * sig * (1.0 + gate * (1.0 - sig))
    grad_up = grad_act * gate * sig
    grads = jnp.concatenate([grad_gate, grad_up], axis=0).astype(BF)

    acts = ring_gather(jnp.concatenate([act, swap(act, "xl")], axis=1))
    own = ring_gather(grads)
    other = [swap(g, "xl") for g in own]
    sums = None
    for k in (0, 7, 1, 6, 2, 5, 3, 4):
        sums = segment_backward(
            where, k, acts[k], own[k], other[k], tok_blocks, cot_blocks, m_gate, m_up, m_down, sums
        )
    out, o_gate, o_up, o_down = sums
    outputs = lax.all_to_all(
        out.reshape(2 * segs, tok, 2 * width), COL, split_axis=0, concat_axis=0, tiled=True
    )
    outputs = jnp.sum(outputs.astype(F32), axis=0).astype(BF)
    merge_grad = route_products((o_gate, o_up, o_down), (gate_weight, up_weight, down_weight))
    grad_route = route_gradient(total_over_all(merge_grad), keep)
    return outputs[:, :width], outputs[:, width:], grad_route


def solution(mesh):
    split = Mesh(mesh.devices.reshape(NZ, 2, 2, 4, 2), SEQ + COL)
    return jax.shard_map(
        on_device,
        mesh=split,
        in_specs=(
            P(SEQ, None),
            P(None, SEQ, COL),
            P(None, SEQ, COL),
            P(None, COL, SEQ),
            P(None, SEQ),
            P(),
            P(),
        ),
        out_specs=(P(COL, SEQ), P(COL, SEQ), P()),
        check_vma=False,
    )
```

```python
import jax
import jax.numpy as jnp
from jax import lax
from jax.experimental import pallas as pl
from jax.experimental.pallas import tpu as pltpu
from jax.sharding import Mesh, PartitionSpec as P

SEQ = ("z", "xl")
COL = ("xh", "y", "core")
NZ = 8
TILE = 32
ROWS = 128
EXTRA = 16
BF = jnp.bfloat16
F32 = jnp.float32


def routing(route, doc_start):
    own = route.astype(F32) / 1024.0
    prev = jnp.concatenate([own[:1], own[:-1]], axis=0)
    first = jnp.arange(route.shape[0]) == 0
    keep = jnp.logical_or(first, doc_start == 1)
    return jnp.where(keep[:, None], own, prev), keep


def route_gradient(merge_grad, keep):
    own_part = jnp.where(keep[:, None], merge_grad, jnp.float32(0.0))
    next_part = jnp.where(keep[:, None], jnp.float32(0.0), merge_grad)
    next_part = jnp.concatenate([next_part[1:], jnp.zeros_like(next_part[:1])], axis=0)
    return (own_part + next_part) / 1024.0


def dot(a, b, ca, cb):
    return lax.dot_general(a, b, (((ca,), (cb,)), ((), ())), preferred_element_type=F32)


def params(mib):
    return pltpu.CompilerParams(vmem_limit_bytes=mib * 1024 * 1024)


def cost(flops, nbytes):
    return pl.CostEstimate(flops=flops, bytes_accessed=nbytes, transcendentals=0)


def by_width(rows, width):
    n = rows.shape[1] // width

    def kernel(rows_r, out):
        for i in range(n):
            out[i] = rows_r[:, i * width : (i + 1) * width]

    return pl.pallas_call(
        kernel,
        out_shape=jax.ShapeDtypeStruct((n, rows.shape[0], width), rows.dtype),
        compiler_params=params(20),
        cost_estimate=cost(0, 4 * rows.size),
        name="by_width",
    )(rows)


def merge_kernel(n, *refs):
    table = refs[0][...]
    experts, rows, width = refs[1].shape
    for w, out in zip(refs[1 : 1 + n], refs[1 + n :]):
        for j in range(0, rows, TILE):
            tile = w[:, j : j + TILE, :].reshape(experts * TILE, width)
            out[:, j : j + TILE, :] = dot(table, tile, 1, 0).astype(BF).reshape(experts, TILE, width)


def merge(table, *weights):
    n = len(weights)
    experts, rows, width = weights[0].shape
    size = weights[0].size
    block = pl.BlockSpec((experts, ROWS, width), lambda i: (0, i, 0))
    return pl.pallas_call(
        lambda *refs: merge_kernel(n, *refs),
        grid=(pl.cdiv(rows, ROWS),),
        in_specs=[pl.BlockSpec(table.shape, lambda i: (0, 0))] + [block] * n,
        out_specs=[block] * n,
        out_shape=[jax.ShapeDtypeStruct(w.shape, BF) for w in weights],
        compiler_params=params(24),
        cost_estimate=cost(2 * 256 * n * size, 4 * n * size),
        name="merge",
    )(table, *weights)


def at_segment(k):
    return lambda i, s: (lax.rem(s[0] + k, NZ), 0, 0)


def at_own(k):
    return lambda i, s: (2 * lax.rem(s[0] + k, NZ) + s[1], 0, 0)


def at_other(k):
    return lambda i, s: (2 * lax.rem(s[0] + k, NZ) + 1 - s[1], 0, 0)


def whole(shape):
    return pl.BlockSpec(shape, lambda i, s: (0,) * len(shape))


def partial_products(where, groups, mats, blocks, front, after=()):
    groups = [g if isinstance(g, tuple) else (g,) for g in groups]
    ks = [k for g in groups for k in g]
    place = [(g, i) for g, ks_of in enumerate(groups) for i in range(len(ks_of))]
    rows, width = mats[0].shape[1:]
    tok = blocks.shape[1]
    n = len(mats)
    per = n + 2
    back = n * rows - front
    specs = []
    args = []
    for k in ks:
        specs += [pl.BlockSpec((1, rows, width), at_segment(k))] * n
        specs += [pl.BlockSpec((1, tok, width), at_own(k)), pl.BlockSpec((1, tok, width), at_other(k))]
        args += list(mats) + [blocks, blocks]
    specs += [pl.BlockSpec(memory_space=pl.ANY)] * len(after)
    shapes = []
    if front:
        shapes = [jax.ShapeDtypeStruct((len(g), front, tok), BF) for g in groups]
        shapes += [jax.ShapeDtypeStruct((front, tok), F32)] * len(ks)
    if back:
        shapes += [jax.ShapeDtypeStruct((back, 2 * tok), F32)] * len(ks)

    def kernel(s_ref, *refs):
        outs = refs[per * len(ks) + len(after) :]
        for i in range(len(ks)):
            part = refs[per * i : per * (i + 1)]
            both = jnp.concatenate([part[n][0], part[n + 1][0]], axis=0)
            for m in range(n):
                r = dot(part[m][0], both, 1, 1)
                at = m * rows
                cut = min(max(front - at, 0), rows)
                if cut:
                    outs[place[i][0]][place[i][1], at : at + cut, :] = r[:cut, tok:].astype(BF)
                    outs[len(groups) + i][at : at + cut, :] = r[:cut, :tok]
                if cut < rows:
                    outs[len(shapes) - len(ks) + i][at + cut - front : at + rows - front, :] = r[cut:, :]

    found = pl.pallas_call(
        kernel,
        grid_spec=pltpu.PrefetchScalarGridSpec(
            num_scalar_prefetch=1,
            grid=(1,),
            in_specs=specs,
            out_specs=[whole(s.shape) for s in shapes],
        ),
        out_shape=shapes,
        compiler_params=params(40),
        cost_estimate=cost(4 * len(ks) * n * rows * width * tok, 8 * len(ks) * n * rows * width),
        name="products",
    )(where, *args, *after)
    g = len(groups) if front else 0
    n = len(ks) if front else 0
    return found[:g], dict(zip(ks, found[g : g + n])), dict(zip(ks, found[g + n :]))


def diagonal(n):
    return lax.broadcasted_iota(jnp.int32, (n, 128), 0) == lax.broadcasted_iota(jnp.int32, (n, 128), 1)


def in_terms(x):
    terms = []
    for _ in range(3):
        terms.append(x.astype(BF).astype(F32))
        x = x - terms[-1]
    return terms + [jnp.zeros_like(x)]


def pack(keep, came, routes):
    segs, tok, width = keep.shape

    def kernel(keep_r, came_r, routes_r, out):
        at = lax.broadcasted_iota(jnp.int32, (segs, 128), 0)
        table = jnp.zeros((segs, 128), F32)
        for d in range(segs):
            out[d, :tok, :] = (keep_r[d] + came_r[d, :tok, :].astype(F32)).astype(BF)
            tail = came_r[d, tok:, :].astype(F32)
            row = routes_r[d, :1, :] + (tail[:1, :128] + tail[:1, 128:256] + tail[:1, 256:384])
            table = jnp.where(at == d, row, table)
        extra = jnp.concatenate(in_terms(table), axis=1)
        extra = jnp.concatenate([extra, jnp.zeros_like(extra)], axis=0).astype(BF)
        for d in range(segs):
            out[d, tok:, :] = extra

    return pl.pallas_call(
        kernel,
        out_shape=jax.ShapeDtypeStruct(came.shape, BF),
        compiler_params=params(20),
        cost_estimate=cost(2 * keep.size, 8 * keep.size),
        name="pack",
    )(keep, came, routes)


def segment_backward(where, k, act, own, other, tok_blocks, cot_blocks, merged, weights, so_far):
    segs, rows, width = merged[0].shape
    tok = tok_blocks.shape[1]

    def kernel(s_ref, act_r, own_r, oth_r, to_r, tp_r, co_r, cp_r, g_r, u_r, d_r, wg_r, wu_r, wd_r, *rest):
        keep, send, route, o_gate, o_up, o_down = rest[-6:]
        a = act_r[...]
        gg = jnp.concatenate([own_r[:rows, :], oth_r[:rows, :]], axis=1)
        gu = jnp.concatenate([own_r[rows:, :], oth_r[rows:, :]], axis=1)
        tokens = jnp.concatenate([to_r[0], tp_r[0]], axis=0)
        cots = jnp.concatenate([co_r[0], cp_r[0]], axis=0)
        o_gate[...] = dot(gg, tokens, 1, 0).astype(BF)
        o_up[...] = dot(gu, tokens, 1, 0).astype(BF)
        o_down[...] = dot(a, cots, 1, 0).astype(BF)
        result = jnp.concatenate([dot(a, d_r[0], 0, 0), dot(gg, g_r[0], 0, 0) + dot(gu, u_r[0], 0, 0)], axis=1)

        @pl.when(s_ref[2] == 0)
        def _():
            keep[0] = result[:tok]
            send[0, :tok, :] = result[tok:].astype(BF)

        @pl.when(s_ref[2] == 1)
        def _():
            keep[0] = result[tok:]
            send[0, :tok, :] = result[:tok].astype(BF)

        def step(j, total):
            at = pl.ds(pl.multiple_of(j * 16, 16), 16)
            p = o_gate[at, :].astype(F32) * wg_r[:, at, :].astype(F32)
            p += o_up[at, :].astype(F32) * wu_r[:, at, :].astype(F32)
            p += o_down[at, :].astype(F32) * wd_r[:, at, :].astype(F32)
            return total + (p[:, :8, :] + p[:, 8:, :])

        total = lax.fori_loop(0, rows // 16, step, jnp.zeros((segs, 8, width), F32))
        sums = jnp.sum(jnp.sum(total, axis=1), axis=1, keepdims=True)
        row = jnp.sum(jnp.where(diagonal(segs), sums, 0.0), axis=0, keepdims=True)
        route[0] = jnp.broadcast_to(row, (8, 128))
        send[0, tok:, :] = jnp.broadcast_to(jnp.concatenate(in_terms(row), axis=1), (EXTRA, 4 * 128)).astype(BF)

    shapes = [
        jax.ShapeDtypeStruct((segs, tok, 2 * width), F32),
        jax.ShapeDtypeStruct((segs, tok + EXTRA, 2 * width), BF),
        jax.ShapeDtypeStruct((segs, 8, 128), F32),
    ]
    seg = pl.BlockSpec((1, rows, width), at_segment(k))
    specs = [
        whole(act.shape),
        whole(own.shape),
        whole(other.shape),
        pl.BlockSpec((1, tok, width), at_own(k)),
        pl.BlockSpec((1, tok, width), at_other(k)),
        pl.BlockSpec((1, tok, width), at_own(k)),
        pl.BlockSpec((1, tok, width), at_other(k)),
        seg,
        seg,
        seg,
    ]
    specs += [pl.BlockSpec(memory_space=pltpu.VMEM)] * 3
    args = [act, own, other, tok_blocks, tok_blocks, cot_blocks, cot_blocks, *merged, *weights]
    aliases = {}
    if so_far is not None:
        aliases = {1 + len(args) + i: i for i in range(3)}
        specs += [pl.BlockSpec(memory_space=pl.ANY)] * 3
        args += list(so_far)
    return pl.pallas_call(
        kernel,
        grid_spec=pltpu.PrefetchScalarGridSpec(
            num_scalar_prefetch=1,
            grid=(1,),
            in_specs=specs,
            out_specs=[pl.BlockSpec((1,) + x.shape[1:], at_segment(k)) for x in shapes],
            scratch_shapes=[pltpu.VMEM((rows, width), BF)] * 3,
        ),
        out_shape=shapes,
        input_output_aliases=aliases,
        compiler_params=params(24),
        cost_estimate=cost(24 * rows * width * tok, 20 * rows * width),
        name="backward",
    )(where, *args)


def shift(x, axis, n, by):
    return lax.ppermute(x, axis, [(i, (i + by) % n) for i in range(n)])


def swap(x, axis):
    return shift(x, axis, 2, 1)


def add(a, b):
    return a.astype(F32) + b.astype(F32)


def middle(rows):
    return rows // 2 // 16 * 16


def both_ways(up, down):
    return shift(up, "z", NZ, 1), shift(down, "z", NZ, -1)


def ring_sum(blocks):
    half = middle(blocks[4].shape[0])
    up, down = both_ways(blocks[4][:half].astype(BF), blocks[4][half:].astype(BF))
    up = jnp.concatenate([add(up, blocks[3][:half]), blocks[3][half:]], axis=0).astype(BF)
    down = jnp.concatenate([blocks[5][:half], add(down, blocks[5][half:])], axis=0).astype(BF)
    up, down = both_ways(up, down)
    up, down = both_ways(add(up, blocks[2]).astype(BF), add(down, blocks[6]).astype(BF))
    up, down = both_ways(add(up, blocks[1]).astype(BF), add(down, blocks[7]).astype(BF))
    return add(up, down) + blocks[0]


def ring_gather(block):
    found = {0: block}
    up = down = block
    for step in range(1, 4):
        up, down = both_ways(up, down)
        found[NZ - step], found[step] = up, down
    half = middle(block.shape[0])
    found[4] = jnp.concatenate(both_ways(up[:half], down[half:]), axis=0)
    return [found[k] for k in range(NZ)]


def sum_of_four(x, axis, n, bits):
    got = [lax.ppermute(x, axis, [(i, i ^ k) for i in range(n)]) for k in bits]
    return (x + got[0]) + (got[1] + got[2])


def on_device(tokens, gate_weight, up_weight, down_weight, cotangent, route, doc_start):
    tok, width_all = tokens.shape
    experts, width, cols = gate_weight.shape
    segs = route.shape[0]
    n_seq = 2 * NZ
    z, xl, core = (lax.axis_index(a).astype(jnp.int32) for a in ("z", "xl", "core"))
    where = jnp.stack([z, xl, (xl + core) % 2])
    used, keep = routing(route, doc_start)
    table = used.astype(BF)[:, None, :, None] * jnp.eye(TILE, dtype=BF)[None, :, None, :]
    table = table.reshape(segs * TILE, experts * TILE)

    tok_blocks = lax.all_to_all(by_width(tokens, width), SEQ, split_axis=0, concat_axis=0, tiled=True)
    cot_blocks = cotangent.reshape(n_seq, tok, width)
    gate_weight = gate_weight.swapaxes(1, 2)
    up_weight = up_weight.swapaxes(1, 2)

    (m_down,) = merge(table, down_weight)
    m_gate, m_up = merge(table, gate_weight, up_weight)

    order = (4, 3, 5, 2, 6, 1, 7, 0)
    _, _, acting = partial_products(where, order, (m_down,), cot_blocks, 0)
    both = ring_sum(acting)
    grad_act = both[:, :tok] + swap(both[:, tok:].astype(BF), "xl").astype(F32)

    groups = ((4, 3, 5), (2, 6), (1, 7), (0,))
    sent, kept, _ = partial_products(where, groups, (m_gate, m_up), tok_blocks, 2 * cols, after=(acting[4],))
    parts = {}
    for ks, block in zip(groups, sent):
        came = swap(block, "xl")
        for i, k in enumerate(ks):
            parts[k] = add(kept[k], came[i])
    pre = ring_sum(parts)

    gate, up = pre[:cols], pre[cols:]
    sig = jax.nn.sigmoid(gate)
    act = (gate * sig * up).astype(BF)
    grad_gate = grad_act * up * sig * (1.0 + gate * (1.0 - sig))
    grad_up = grad_act * gate * sig
    grads = jnp.concatenate([grad_gate, grad_up], axis=0).astype(BF)

    act_other = swap(act, "xl")
    own = ring_gather(grads)
    other = {}
    for ks in ((0,), (7, 1), (6, 2), (5, 3), (4,)):
        if len(ks) == 1:
            other[ks[0]] = swap(own[ks[0]], "xl")
        else:
            came = swap(jnp.stack([own[k] for k in ks]), "xl")
            other.update({k: came[i] for i, k in enumerate(ks)})
    act_both, _ = lax.optimization_barrier((jnp.concatenate([act, act_other], axis=1), own[7]))
    acts = ring_gather(act_both)
    sums = None
    for k in (0, 7, 1, 6, 2, 5, 3, 4):
        sums = segment_backward(
            where,
            k,
            acts[k],
            own[k],
            other[k],
            tok_blocks,
            cot_blocks,
            (m_gate, m_up, m_down),
            (gate_weight, up_weight, down_weight),
            sums,
        )
    partial, sent, routes = sums
    packed = pack(partial, swap(sent, "core"), routes)
    got = lax.all_to_all(packed, ("xh", "y"), split_axis=0, concat_axis=0, tiled=True).astype(F32)
    outputs = jnp.sum(got[:, :tok], axis=0).astype(BF)
    extra = jnp.sum(got[:, tok : tok + segs], axis=0)
    merge_grad = sum(extra[:, 128 * i : 128 * i + experts] for i in range(3))
    merge_grad = sum_of_four(merge_grad, SEQ, 2 * NZ, (1, 8, 9))
    merge_grad = sum_of_four(merge_grad, SEQ, 2 * NZ, (2, 4, 6))
    grad_route = route_gradient(merge_grad, keep)
    return outputs[:, :width], outputs[:, width:], grad_route


def solution(mesh):
    split = Mesh(mesh.devices.reshape(NZ, 2, 2, 4, 2), SEQ + COL)
    return jax.shard_map(
        on_device,
        mesh=split,
        in_specs=(
            P(SEQ, None),
            P(None, SEQ, COL),
            P(None, SEQ, COL),
            P(None, COL, SEQ),
            P(None, SEQ),
            P(),
            P(),
        ),
        out_specs=(P(COL, SEQ), P(COL, SEQ), P()),
        check_vma=False,
    )
```

```python
import jax
import jax.numpy as jnp
from jax import lax
from jax.experimental import pallas as pl
from jax.experimental.pallas import tpu as pltpu
from jax.sharding import Mesh, PartitionSpec as P

SEQ = ("z", "xl")
COL = ("xh", "y", "core")
NZ = 8
TILE = 32
ROWS = 128
EXTRA = 16
BF = jnp.bfloat16
F32 = jnp.float32


def routing(route, doc_start):
    own = route.astype(F32) / 1024.0
    prev = jnp.concatenate([own[:1], own[:-1]], axis=0)
    first = jnp.arange(route.shape[0]) == 0
    keep = jnp.logical_or(first, doc_start == 1)
    return jnp.where(keep[:, None], own, prev), keep


def route_gradient(merge_grad, keep):
    own_part = jnp.where(keep[:, None], merge_grad, jnp.float32(0.0))
    next_part = jnp.where(keep[:, None], jnp.float32(0.0), merge_grad)
    next_part = jnp.concatenate([next_part[1:], jnp.zeros_like(next_part[:1])], axis=0)
    return (own_part + next_part) / 1024.0


def dot(a, b, ca, cb):
    return lax.dot_general(a, b, (((ca,), (cb,)), ((), ())), preferred_element_type=F32)


def params(mib):
    return pltpu.CompilerParams(vmem_limit_bytes=mib * 1024 * 1024)


def cost(flops, nbytes):
    return pl.CostEstimate(flops=flops, bytes_accessed=nbytes, transcendentals=0)


def by_width(rows, width):
    n = rows.shape[1] // width

    def kernel(rows_r, out):
        for i in range(n):
            out[i] = rows_r[:, i * width : (i + 1) * width]

    return pl.pallas_call(
        kernel,
        out_shape=jax.ShapeDtypeStruct((n, rows.shape[0], width), rows.dtype),
        compiler_params=params(20),
        cost_estimate=cost(0, 4 * rows.size),
        name="by_width",
    )(rows)


def merge_kernel(n, *refs):
    table = refs[0][...]
    experts, rows, width = refs[1].shape
    for w, out in zip(refs[1 : 1 + n], refs[1 + n :]):
        for j in range(0, rows, TILE):
            tile = w[:, j : j + TILE, :].reshape(experts * TILE, width)
            out[:, j : j + TILE, :] = dot(table, tile, 1, 0).astype(BF).reshape(experts, TILE, width)


def merge(table, *weights):
    n = len(weights)
    experts, rows, width = weights[0].shape
    size = weights[0].size
    block = pl.BlockSpec((experts, ROWS, width), lambda i: (0, i, 0))
    return pl.pallas_call(
        lambda *refs: merge_kernel(n, *refs),
        grid=(pl.cdiv(rows, ROWS),),
        in_specs=[pl.BlockSpec(table.shape, lambda i: (0, 0))] + [block] * n,
        out_specs=[block] * n,
        out_shape=[pltpu.HBM(w.shape, BF) for w in weights],
        compiler_params=params(24),
        cost_estimate=cost(2 * 256 * n * size, 4 * n * size),
        name="merge",
    )(table, *weights)


def at_segment(k):
    return lambda i, s: (lax.rem(s[0] + k, NZ), 0, 0)


def at_own(k):
    return lambda i, s: (2 * lax.rem(s[0] + k, NZ) + s[1], 0, 0)


def at_other(k):
    return lambda i, s: (2 * lax.rem(s[0] + k, NZ) + 1 - s[1], 0, 0)


def whole(shape):
    return pl.BlockSpec(shape, lambda i, s: (0,) * len(shape))


def partial_products(where, groups, mats, blocks, front, after=()):
    groups = [g if isinstance(g, tuple) else (g,) for g in groups]
    ks = [k for g in groups for k in g]
    place = [(g, i) for g, ks_of in enumerate(groups) for i in range(len(ks_of))]
    rows, width = mats[0].shape[1:]
    tok = blocks.shape[1]
    n = len(mats)
    per = n + 2
    back = n * rows - front
    specs = []
    args = []
    for k in ks:
        specs += [pl.BlockSpec((1, rows, width), at_segment(k))] * n
        specs += [pl.BlockSpec((1, tok, width), at_own(k)), pl.BlockSpec((1, tok, width), at_other(k))]
        args += list(mats) + [blocks, blocks]
    specs += [pl.BlockSpec(memory_space=pl.ANY)] * len(after)
    shapes = []
    if front:
        shapes = [jax.ShapeDtypeStruct((len(g), front, tok), BF) for g in groups]
        shapes += [jax.ShapeDtypeStruct((front, tok), F32)] * len(ks)
    if back:
        shapes += [jax.ShapeDtypeStruct((back, 2 * tok), F32)] * len(ks)

    def kernel(s_ref, *refs):
        outs = refs[per * len(ks) + len(after) :]
        for i in range(len(ks)):
            part = refs[per * i : per * (i + 1)]
            both = jnp.concatenate([part[n][0], part[n + 1][0]], axis=0)
            for m in range(n):
                r = dot(part[m][0], both, 1, 1)
                at = m * rows
                cut = min(max(front - at, 0), rows)
                if cut:
                    outs[place[i][0]][place[i][1], at : at + cut, :] = r[:cut, tok:].astype(BF)
                    outs[len(groups) + i][at : at + cut, :] = r[:cut, :tok]
                if cut < rows:
                    outs[len(shapes) - len(ks) + i][at + cut - front : at + rows - front, :] = r[cut:, :]

    found = pl.pallas_call(
        kernel,
        grid_spec=pltpu.PrefetchScalarGridSpec(
            num_scalar_prefetch=1,
            grid=(1,),
            in_specs=specs,
            out_specs=[whole(s.shape) for s in shapes],
        ),
        out_shape=shapes,
        compiler_params=params(40),
        cost_estimate=cost(4 * len(ks) * n * rows * width * tok, 8 * len(ks) * n * rows * width),
        name="products",
    )(where, *args, *after)
    g = len(groups) if front else 0
    n = len(ks) if front else 0
    return found[:g], dict(zip(ks, found[g : g + n])), dict(zip(ks, found[g + n :]))


def diagonal(n):
    return lax.broadcasted_iota(jnp.int32, (n, 128), 0) == lax.broadcasted_iota(jnp.int32, (n, 128), 1)


def in_terms(x):
    terms = []
    for _ in range(3):
        terms.append(x.astype(BF).astype(F32))
        x = x - terms[-1]
    return terms + [jnp.zeros_like(x)]


def pack(keep, came, routes):
    segs, tok, width = keep.shape

    def kernel(keep_r, came_r, routes_r, out):
        at = lax.broadcasted_iota(jnp.int32, (segs, 128), 0)
        table = jnp.zeros((segs, 128), F32)
        for d in range(segs):
            out[d, :tok, :] = (keep_r[d] + came_r[d, :tok, :].astype(F32)).astype(BF)
            tail = came_r[d, tok:, :].astype(F32)
            row = routes_r[d, :1, :] + (tail[:1, :128] + tail[:1, 128:256] + tail[:1, 256:384])
            table = jnp.where(at == d, row, table)
        extra = jnp.concatenate(in_terms(table), axis=1)
        extra = jnp.concatenate([extra, jnp.zeros_like(extra)], axis=0).astype(BF)
        for d in range(segs):
            out[d, tok:, :] = extra

    return pl.pallas_call(
        kernel,
        out_shape=jax.ShapeDtypeStruct(came.shape, BF),
        compiler_params=params(20),
        cost_estimate=cost(2 * keep.size, 8 * keep.size),
        name="pack",
    )(keep, came, routes)


def segment_backward(where, k, act, own, other, tok_blocks, cot_blocks, merged, weights, so_far):
    segs, rows, width = merged[0].shape
    tok = tok_blocks.shape[1]

    def kernel(s_ref, act_r, own_r, oth_r, to_r, tp_r, co_r, cp_r, g_r, u_r, d_r, wg_r, wu_r, wd_r, *rest):
        keep, send, route, o_gate, o_up, o_down = rest[-6:]
        a = act_r[...]
        gg = jnp.concatenate([own_r[:rows, :], oth_r[:rows, :]], axis=1)
        gu = jnp.concatenate([own_r[rows:, :], oth_r[rows:, :]], axis=1)
        tokens = jnp.concatenate([to_r[0], tp_r[0]], axis=0)
        cots = jnp.concatenate([co_r[0], cp_r[0]], axis=0)
        o_gate[...] = dot(gg, tokens, 1, 0).astype(BF)
        o_up[...] = dot(gu, tokens, 1, 0).astype(BF)
        o_down[...] = dot(a, cots, 1, 0).astype(BF)
        result = jnp.concatenate([dot(a, d_r[0], 0, 0), dot(gg, g_r[0], 0, 0) + dot(gu, u_r[0], 0, 0)], axis=1)

        @pl.when(s_ref[2] == 0)
        def _():
            keep[0] = result[:tok]
            send[0, :tok, :] = result[tok:].astype(BF)

        @pl.when(s_ref[2] == 1)
        def _():
            keep[0] = result[tok:]
            send[0, :tok, :] = result[:tok].astype(BF)

        def step(j, total):
            at = pl.ds(pl.multiple_of(j * 16, 16), 16)
            p = o_gate[at, :].astype(F32) * wg_r[:, at, :].astype(F32)
            p += o_up[at, :].astype(F32) * wu_r[:, at, :].astype(F32)
            p += o_down[at, :].astype(F32) * wd_r[:, at, :].astype(F32)
            return total + (p[:, :8, :] + p[:, 8:, :])

        total = lax.fori_loop(0, rows // 16, step, jnp.zeros((segs, 8, width), F32))
        sums = jnp.sum(jnp.sum(total, axis=1), axis=1, keepdims=True)
        row = jnp.sum(jnp.where(diagonal(segs), sums, 0.0), axis=0, keepdims=True)
        route[0] = jnp.broadcast_to(row, (8, 128))
        send[0, tok:, :] = jnp.broadcast_to(jnp.concatenate(in_terms(row), axis=1), (EXTRA, 4 * 128)).astype(BF)

    shapes = [
        jax.ShapeDtypeStruct((segs, tok, 2 * width), F32),
        jax.ShapeDtypeStruct((segs, tok + EXTRA, 2 * width), BF),
        jax.ShapeDtypeStruct((segs, 8, 128), F32),
    ]
    seg = pl.BlockSpec((1, rows, width), at_segment(k))
    specs = [
        whole(act.shape),
        whole(own.shape),
        whole(other.shape),
        pl.BlockSpec((1, tok, width), at_own(k)),
        pl.BlockSpec((1, tok, width), at_other(k)),
        pl.BlockSpec((1, tok, width), at_own(k)),
        pl.BlockSpec((1, tok, width), at_other(k)),
        seg,
        seg,
        seg,
    ]
    specs += [pl.BlockSpec(memory_space=pltpu.VMEM)] * 3
    args = [act, own, other, tok_blocks, tok_blocks, cot_blocks, cot_blocks, *merged, *weights]
    aliases = {}
    if so_far is not None:
        aliases = {1 + len(args) + i: i for i in range(3)}
        specs += [pl.BlockSpec(memory_space=pl.ANY)] * 3
        args += list(so_far)
    return pl.pallas_call(
        kernel,
        grid_spec=pltpu.PrefetchScalarGridSpec(
            num_scalar_prefetch=1,
            grid=(1,),
            in_specs=specs,
            out_specs=[pl.BlockSpec((1,) + x.shape[1:], at_segment(k)) for x in shapes],
            scratch_shapes=[pltpu.VMEM((rows, width), BF)] * 3,
        ),
        out_shape=shapes,
        input_output_aliases=aliases,
        compiler_params=params(24),
        cost_estimate=cost(24 * rows * width * tok, 20 * rows * width),
        name="backward",
    )(where, *args)


def shift(x, axis, n, by):
    return lax.ppermute(x, axis, [(i, (i + by) % n) for i in range(n)])


def swap(x, axis):
    return shift(x, axis, 2, 1)


def add(a, b):
    return a.astype(F32) + b.astype(F32)


def middle(rows):
    return rows // 2 // 16 * 16


def both_ways(up, down):
    return shift(up, "z", NZ, 1), shift(down, "z", NZ, -1)


def ring_sum(blocks):
    half = middle(blocks[4].shape[0])
    up, down = both_ways(blocks[4][:half].astype(BF), blocks[4][half:].astype(BF))
    up = jnp.concatenate([add(up, blocks[3][:half]), blocks[3][half:]], axis=0).astype(BF)
    down = jnp.concatenate([blocks[5][:half], add(down, blocks[5][half:])], axis=0).astype(BF)
    up, down = both_ways(up, down)
    up, down = both_ways(add(up, blocks[2]).astype(BF), add(down, blocks[6]).astype(BF))
    up, down = both_ways(add(up, blocks[1]).astype(BF), add(down, blocks[7]).astype(BF))
    return add(up, down) + blocks[0]


def ring_gather(block):
    found = {0: block}
    up = down = block
    for step in range(1, 4):
        up, down = both_ways(up, down)
        found[NZ - step], found[step] = up, down
    half = middle(block.shape[0])
    found[4] = jnp.concatenate(both_ways(up[:half], down[half:]), axis=0)
    return [found[k] for k in range(NZ)]


def on_device(tokens, gate_weight, up_weight, down_weight, cotangent, route, doc_start):
    tok, width_all = tokens.shape
    experts, width, cols = gate_weight.shape
    segs = route.shape[0]
    n_seq = 2 * NZ
    z, xl, core = (lax.axis_index(a).astype(jnp.int32) for a in ("z", "xl", "core"))
    where = jnp.stack([z, xl, (xl + core) % 2])
    used, keep = routing(route, doc_start)
    table = used.astype(BF)[:, None, :, None] * jnp.eye(TILE, dtype=BF)[None, :, None, :]
    table = table.reshape(segs * TILE, experts * TILE)

    tok_blocks = lax.all_to_all(by_width(tokens, width), SEQ, split_axis=0, concat_axis=0, tiled=True)
    cot_blocks = cotangent.reshape(n_seq, tok, width)
    gate_weight = gate_weight.swapaxes(1, 2)
    up_weight = up_weight.swapaxes(1, 2)

    (m_down,) = merge(table, down_weight)
    m_gate, m_up = merge(table, gate_weight, up_weight)

    order = (4, 3, 5, 2, 6, 1, 7, 0)
    _, _, acting = partial_products(where, order, (m_down,), cot_blocks, 0)
    both = ring_sum(acting)
    grad_act = both[:, :tok] + swap(both[:, tok:].astype(BF), "xl").astype(F32)

    first, later = ((4, 3, 5),), ((2, 6), (1, 7), (0,))
    mats = (m_gate, m_up)
    sends, kept, _ = partial_products(where, first, mats, tok_blocks, 2 * cols, after=(acting[4],))
    came = [swap(sends[0], "xl")]
    sends, more, _ = partial_products(where, later, mats, tok_blocks, 2 * cols, after=(acting[4],))
    came[0], *sends = lax.optimization_barrier((came[0], *sends))
    came += [swap(block, "xl") for block in sends]
    kept.update(more)
    parts = {}
    for ks, block in zip(first + later, came):
        for i, k in enumerate(ks):
            parts[k] = add(kept[k], block[i])
    pre = ring_sum(parts)

    gate, up = pre[:cols], pre[cols:]
    sig = jax.nn.sigmoid(gate)
    act = (gate * sig * up).astype(BF)
    grad_gate = grad_act * up * sig * (1.0 + gate * (1.0 - sig))
    grad_up = grad_act * gate * sig
    grads = jnp.concatenate([grad_gate, grad_up], axis=0).astype(BF)

    act_and_grads = jnp.concatenate([act, grads], axis=0)
    came = swap(act_and_grads, "xl")
    other = {0: came[cols:]}
    own = ring_gather(grads)
    for ks in ((7, 1), (6, 2), (5, 3)):
        pair = swap(jnp.stack([own[k] for k in ks]), "xl")
        other.update({k: pair[i] for i, k in enumerate(ks)})
    other[4] = swap(own[4], "xl")
    act_both, _ = lax.optimization_barrier((jnp.concatenate([act, came[:cols]], axis=1), own[7]))
    acts = ring_gather(act_both)
    sums = None
    for k in (0, 7, 1, 6, 2, 5, 3, 4):
        sums = segment_backward(
            where,
            k,
            acts[k],
            own[k],
            other[k],
            tok_blocks,
            cot_blocks,
            (m_gate, m_up, m_down),
            (gate_weight, up_weight, down_weight),
            sums,
        )
    partial, sent, routes = sums
    packed = pack(partial, swap(sent, "core"), routes)
    got = lax.all_to_all(packed, ("xh", "y"), split_axis=0, concat_axis=0, tiled=True).astype(F32)
    outputs = jnp.sum(got[:, :tok], axis=0).astype(BF)
    extra = jnp.sum(got[:, tok : tok + segs], axis=0)
    merge_grad = sum(extra[:, 128 * i : 128 * i + experts] for i in range(3))
    copies = jnp.broadcast_to(merge_grad[None], (n_seq, segs, experts))
    merge_grad = jnp.sum(lax.all_to_all(copies, SEQ, split_axis=0, concat_axis=0, tiled=True), axis=0)
    grad_route = route_gradient(merge_grad, keep)
    return outputs[:, :width], outputs[:, width:], grad_route


def solution(mesh):
    split = Mesh(mesh.devices.reshape(NZ, 2, 2, 4, 2), SEQ + COL)
    return jax.shard_map(
        on_device,
        mesh=split,
        in_specs=(
            P(SEQ, None),
            P(None, SEQ, COL),
            P(None, SEQ, COL),
            P(None, COL, SEQ),
            P(None, SEQ),
            P(),
            P(),
        ),
        out_specs=(P(COL, SEQ), P(COL, SEQ), P()),
        check_vma=False,
    )
```

```python
import jax
import jax.numpy as jnp
from jax import lax
from jax.experimental import pallas as pl
from jax.experimental.pallas import tpu as pltpu
from jax.sharding import Mesh, PartitionSpec as P

SEQ = ("z", "xl")
COL = ("xh", "y", "core")
NZ = 8
TILE = 32
ROWS = 128
EXTRA = 16
BF = jnp.bfloat16
F32 = jnp.float32


def routing(route, doc_start):
    own = route.astype(F32) / 1024.0
    prev = jnp.concatenate([own[:1], own[:-1]], axis=0)
    first = jnp.arange(route.shape[0]) == 0
    keep = jnp.logical_or(first, doc_start == 1)
    return jnp.where(keep[:, None], own, prev), keep


def route_gradient(merge_grad, keep):
    own_part = jnp.where(keep[:, None], merge_grad, jnp.float32(0.0))
    next_part = jnp.where(keep[:, None], jnp.float32(0.0), merge_grad)
    next_part = jnp.concatenate([next_part[1:], jnp.zeros_like(next_part[:1])], axis=0)
    return (own_part + next_part) / 1024.0


def dot(a, b, ca, cb):
    return lax.dot_general(a, b, (((ca,), (cb,)), ((), ())), preferred_element_type=F32)


def params(mib):
    return pltpu.CompilerParams(vmem_limit_bytes=mib * 1024 * 1024)


def cost(flops, nbytes):
    return pl.CostEstimate(flops=flops, bytes_accessed=nbytes, transcendentals=0)


def by_width(rows, width):
    n = rows.shape[1] // width

    def kernel(rows_r, out):
        for i in range(n):
            out[i] = rows_r[:, i * width : (i + 1) * width]

    return pl.pallas_call(
        kernel,
        out_shape=jax.ShapeDtypeStruct((n, rows.shape[0], width), rows.dtype),
        compiler_params=params(8),
        cost_estimate=cost(0, 4 * rows.size),
        name="by_width",
    )(rows)


def merge_kernel(n, *refs):
    table = refs[0][...]
    experts, rows, width = refs[1].shape
    for w, out in zip(refs[1 : 1 + n], refs[1 + n :]):
        for j in range(0, rows, TILE):
            tile = w[:, j : j + TILE, :].reshape(experts * TILE, width)
            out[:, j : j + TILE, :] = dot(table, tile, 1, 0).astype(BF).reshape(experts, TILE, width)


def merge(table, *weights):
    n = len(weights)
    experts, rows, width = weights[0].shape
    size = weights[0].size
    block = pl.BlockSpec((experts, ROWS, width), lambda i: (0, i, 0))
    return pl.pallas_call(
        lambda *refs: merge_kernel(n, *refs),
        grid=(pl.cdiv(rows, ROWS),),
        in_specs=[pl.BlockSpec(table.shape, lambda i: (0, 0))] + [block] * n,
        out_specs=[block] * n,
        out_shape=[pltpu.HBM(w.shape, BF) for w in weights],
        compiler_params=params(14),
        cost_estimate=cost(2 * 256 * n * size, 4 * n * size),
        name="merge",
    )(table, *weights)


def at_segment(k):
    return lambda i, s: (lax.rem(s[0] + k, NZ), 0, 0)


def at_own(k):
    return lambda i, s: (2 * lax.rem(s[0] + k, NZ) + s[1], 0, 0)


def at_other(k):
    return lambda i, s: (2 * lax.rem(s[0] + k, NZ) + 1 - s[1], 0, 0)


def whole(shape):
    return pl.BlockSpec(shape, lambda i, s: (0,) * len(shape))


def partial_products(where, groups, mats, blocks, front, after=()):
    groups = [g if isinstance(g, tuple) else (g,) for g in groups]
    ks = [k for g in groups for k in g]
    place = [(g, i) for g, ks_of in enumerate(groups) for i in range(len(ks_of))]
    rows, width = mats[0].shape[1:]
    tok = blocks.shape[1]
    n = len(mats)
    per = n + 2
    back = n * rows - front
    specs = []
    args = []
    for k in ks:
        specs += [pl.BlockSpec((1, rows, width), at_segment(k))] * n
        specs += [pl.BlockSpec((1, tok, width), at_own(k)), pl.BlockSpec((1, tok, width), at_other(k))]
        args += list(mats) + [blocks, blocks]
    specs += [pl.BlockSpec(memory_space=pl.ANY)] * len(after)
    shapes = []
    if front:
        shapes = [jax.ShapeDtypeStruct((len(g), front, tok), BF) for g in groups]
        shapes += [jax.ShapeDtypeStruct((front, tok), F32)] * len(ks)
    if back:
        shapes += [jax.ShapeDtypeStruct((back, 2 * tok), F32)] * len(ks)

    def kernel(s_ref, *refs):
        outs = refs[per * len(ks) + len(after) :]
        for i in range(len(ks)):
            part = refs[per * i : per * (i + 1)]
            both = jnp.concatenate([part[n][0], part[n + 1][0]], axis=0)
            for m in range(n):
                r = dot(part[m][0], both, 1, 1)
                at = m * rows
                cut = min(max(front - at, 0), rows)
                if cut:
                    outs[place[i][0]][place[i][1], at : at + cut, :] = r[:cut, tok:].astype(BF)
                    outs[len(groups) + i][at : at + cut, :] = r[:cut, :tok]
                if cut < rows:
                    outs[len(shapes) - len(ks) + i][at + cut - front : at + rows - front, :] = r[cut:, :]

    found = pl.pallas_call(
        kernel,
        grid_spec=pltpu.PrefetchScalarGridSpec(
            num_scalar_prefetch=1,
            grid=(1,),
            in_specs=specs,
            out_specs=[whole(s.shape) for s in shapes],
        ),
        out_shape=shapes,
        compiler_params=params(24),
        cost_estimate=cost(4 * len(ks) * n * rows * width * tok, 8 * len(ks) * n * rows * width),
        name="products",
    )(where, *args, *after)
    g = len(groups) if front else 0
    n = len(ks) if front else 0
    return found[:g], dict(zip(ks, found[g : g + n])), dict(zip(ks, found[g + n :]))


def diagonal(n):
    return lax.broadcasted_iota(jnp.int32, (n, 128), 0) == lax.broadcasted_iota(jnp.int32, (n, 128), 1)


def in_terms(x):
    terms = []
    for _ in range(3):
        terms.append(x.astype(BF).astype(F32))
        x = x - terms[-1]
    return terms + [jnp.zeros_like(x)]


def pack(keep, came, routes):
    segs, tok, width = keep.shape

    def kernel(keep_r, came_r, routes_r, out):
        at = lax.broadcasted_iota(jnp.int32, (segs, 128), 0)
        table = jnp.zeros((segs, 128), F32)
        for d in range(segs):
            out[d, :tok, :] = (keep_r[d] + came_r[d, :tok, :].astype(F32)).astype(BF)
            tail = came_r[d, tok:, :].astype(F32)
            row = routes_r[d, :1, :] + (tail[:1, :128] + tail[:1, 128:256] + tail[:1, 256:384])
            table = jnp.where(at == d, row, table)
        extra = jnp.concatenate(in_terms(table), axis=1)
        extra = jnp.concatenate([extra, jnp.zeros_like(extra)], axis=0).astype(BF)
        for d in range(segs):
            out[d, tok:, :] = extra

    return pl.pallas_call(
        kernel,
        out_shape=jax.ShapeDtypeStruct(came.shape, BF),
        compiler_params=params(14),
        cost_estimate=cost(2 * keep.size, 8 * keep.size),
        name="pack",
    )(keep, came, routes)


def segment_backward(where, k, act, own, other, tok_blocks, cot_blocks, merged, weights, so_far):
    segs, rows, width = merged[0].shape
    tok = tok_blocks.shape[1]

    def kernel(s_ref, act_r, own_r, oth_r, to_r, tp_r, co_r, cp_r, g_r, u_r, d_r, wg_r, wu_r, wd_r, *rest):
        keep, send, route, o_gate, o_up, o_down = rest[-6:]
        a = act_r[...]
        gg = jnp.concatenate([own_r[:rows, :], oth_r[:rows, :]], axis=1)
        gu = jnp.concatenate([own_r[rows:, :], oth_r[rows:, :]], axis=1)
        tokens = jnp.concatenate([to_r[0], tp_r[0]], axis=0)
        cots = jnp.concatenate([co_r[0], cp_r[0]], axis=0)
        o_gate[...] = dot(gg, tokens, 1, 0).astype(BF)
        o_up[...] = dot(gu, tokens, 1, 0).astype(BF)
        o_down[...] = dot(a, cots, 1, 0).astype(BF)
        result = jnp.concatenate([dot(a, d_r[0], 0, 0), dot(gg, g_r[0], 0, 0) + dot(gu, u_r[0], 0, 0)], axis=1)

        @pl.when(s_ref[2] == 0)
        def _():
            keep[0] = result[:tok]
            send[0, :tok, :] = result[tok:].astype(BF)

        @pl.when(s_ref[2] == 1)
        def _():
            keep[0] = result[tok:]
            send[0, :tok, :] = result[:tok].astype(BF)

        def step(j, total):
            at = pl.ds(pl.multiple_of(j * 16, 16), 16)
            p = o_gate[at, :].astype(F32) * wg_r[:, at, :].astype(F32)
            p += o_up[at, :].astype(F32) * wu_r[:, at, :].astype(F32)
            p += o_down[at, :].astype(F32) * wd_r[:, at, :].astype(F32)
            return total + (p[:, :8, :] + p[:, 8:, :])

        total = lax.fori_loop(0, rows // 16, step, jnp.zeros((segs, 8, width), F32))
        sums = jnp.sum(jnp.sum(total, axis=1), axis=1, keepdims=True)
        row = jnp.sum(jnp.where(diagonal(segs), sums, 0.0), axis=0, keepdims=True)
        route[0] = jnp.broadcast_to(row, (8, 128))
        send[0, tok:, :] = jnp.broadcast_to(jnp.concatenate(in_terms(row), axis=1), (EXTRA, 4 * 128)).astype(BF)

    shapes = [
        jax.ShapeDtypeStruct((segs, tok, 2 * width), F32),
        jax.ShapeDtypeStruct((segs, tok + EXTRA, 2 * width), BF),
        jax.ShapeDtypeStruct((segs, 8, 128), F32),
    ]
    seg = pl.BlockSpec((1, rows, width), at_segment(k))
    specs = [
        whole(act.shape),
        whole(own.shape),
        whole(other.shape),
        pl.BlockSpec((1, tok, width), at_own(k)),
        pl.BlockSpec((1, tok, width), at_other(k)),
        pl.BlockSpec((1, tok, width), at_own(k)),
        pl.BlockSpec((1, tok, width), at_other(k)),
        seg,
        seg,
        seg,
    ]
    specs += [pl.BlockSpec(memory_space=pltpu.VMEM)] * 3
    args = [act, own, other, tok_blocks, tok_blocks, cot_blocks, cot_blocks, *merged, *weights]
    aliases = {}
    if so_far is not None:
        aliases = {1 + len(args) + i: i for i in range(3)}
        specs += [pl.BlockSpec(memory_space=pl.ANY)] * 3
        args += list(so_far)
    return pl.pallas_call(
        kernel,
        grid_spec=pltpu.PrefetchScalarGridSpec(
            num_scalar_prefetch=1,
            grid=(1,),
            in_specs=specs,
            out_specs=[pl.BlockSpec((1,) + x.shape[1:], at_segment(k)) for x in shapes],
            scratch_shapes=[pltpu.VMEM((rows, width), BF)] * 3,
        ),
        out_shape=shapes,
        input_output_aliases=aliases,
        compiler_params=params(14),
        cost_estimate=cost(24 * rows * width * tok, 20 * rows * width),
        name="backward",
    )(where, *args)


def shift(x, axis, n, by):
    return lax.ppermute(x, axis, [(i, (i + by) % n) for i in range(n)])


def swap(x, axis):
    return shift(x, axis, 2, 1)


def add(a, b):
    return a.astype(F32) + b.astype(F32)


def middle(rows):
    return rows // 2 // 16 * 16


def both_ways(up, down):
    return shift(up, "z", NZ, 1), shift(down, "z", NZ, -1)


def ring_sum(blocks):
    half = middle(blocks[4].shape[0])
    up, down = both_ways(blocks[4][:half].astype(BF), blocks[4][half:].astype(BF))
    up = jnp.concatenate([add(up, blocks[3][:half]), blocks[3][half:]], axis=0).astype(BF)
    down = jnp.concatenate([blocks[5][:half], add(down, blocks[5][half:])], axis=0).astype(BF)
    up, down = both_ways(up, down)
    up, down = both_ways(add(up, blocks[2]).astype(BF), add(down, blocks[6]).astype(BF))
    up, down = both_ways(add(up, blocks[1]).astype(BF), add(down, blocks[7]).astype(BF))
    return add(up, down) + blocks[0]


def farthest(up, down):
    half = middle(up.shape[0])
    return jnp.concatenate(both_ways(up[:half], down[half:]), axis=0)


def on_device(tokens, gate_weight, up_weight, down_weight, cotangent, route, doc_start):
    tok, width_all = tokens.shape
    experts, width, cols = gate_weight.shape
    segs = route.shape[0]
    n_seq = 2 * NZ
    z, xl, core = (lax.axis_index(a).astype(jnp.int32) for a in ("z", "xl", "core"))
    where = jnp.stack([z, xl, (xl + core) % 2])
    used, keep = routing(route, doc_start)
    table = used.astype(BF)[:, None, :, None] * jnp.eye(TILE, dtype=BF)[None, :, None, :]
    table = table.reshape(segs * TILE, experts * TILE)

    tok_blocks = lax.all_to_all(by_width(tokens, width), SEQ, split_axis=0, concat_axis=0, tiled=True)
    cot_blocks = cotangent.reshape(n_seq, tok, width)
    gate_weight = gate_weight.swapaxes(1, 2)
    up_weight = up_weight.swapaxes(1, 2)

    (m_down,) = merge(table, down_weight)
    m_gate, m_up = merge(table, gate_weight, up_weight)

    order = (4, 3, 5, 2, 6, 1, 7, 0)
    _, _, acting = partial_products(where, order, (m_down,), cot_blocks, 0)
    both = ring_sum(acting)
    grad_act = both[:, :tok] + swap(both[:, tok:].astype(BF), "xl").astype(F32)

    first, later = ((4, 3, 5),), ((2, 6), (1, 7), (0,))
    mats = (m_gate, m_up)
    sends, kept, _ = partial_products(where, first, mats, tok_blocks, 2 * cols, after=(acting[4],))
    came = [swap(sends[0], "xl")]
    sends, more, _ = partial_products(where, later, mats, tok_blocks, 2 * cols, after=(acting[4],))
    came[0], *sends = lax.optimization_barrier((came[0], *sends))
    came += [swap(block, "xl") for block in sends]
    kept.update(more)
    parts = {}
    for ks, block in zip(first + later, came):
        for i, k in enumerate(ks):
            parts[k] = add(kept[k], block[i])
    pre = ring_sum(parts)

    gate, up = pre[:cols], pre[cols:]
    sig = jax.nn.sigmoid(gate)
    act = (gate * sig * up).astype(BF)
    grad_gate = grad_act * up * sig * (1.0 + gate * (1.0 - sig))
    grad_up = grad_act * gate * sig
    grads = jnp.concatenate([grad_gate, grad_up], axis=0).astype(BF)

    act_and_grads = jnp.concatenate([act, grads], axis=0)
    came = swap(act_and_grads, "xl")
    other = {0: came[cols:]}
    own, acts = {0: grads}, {0: jnp.concatenate([act, came[:cols]], axis=1)}
    sums = None

    def swap_pair(*ks):
        pair = swap(jnp.stack([own[k] for k in ks]), "xl")
        other.update({k: pair[i] for i, k in enumerate(ks)})

    def backward(*ks):
        found = sums
        for k in ks:
            found = segment_backward(
                where,
                k,
                acts[k],
                own[k],
                other[k],
                tok_blocks,
                cot_blocks,
                (m_gate, m_up, m_down),
                (gate_weight, up_weight, down_weight),
                found,
            )
        return found

    own[7], own[1] = both_ways(grads, grads)
    swap_pair(7, 1)
    first_act, _ = lax.optimization_barrier((acts[0], own[7]))
    acts[7], acts[1] = both_ways(first_act, first_act)
    own[6], own[2] = both_ways(own[7], own[1])
    swap_pair(6, 2)
    sums = backward(0, 7, 1)
    up, down = both_ways(own[6], own[2])
    own[5], own[3], _ = lax.optimization_barrier((up, down, sums[2]))
    swap_pair(5, 3)
    own[4] = farthest(own[5], own[3])
    swap_pair(4)
    acts[6], acts[2] = both_ways(acts[7], acts[1])
    acts[5], acts[3] = both_ways(acts[6], acts[2])
    acts[4] = farthest(acts[5], acts[3])
    sums = backward(6, 2, 5, 3, 4)
    partial, sent, routes = sums
    packed = pack(partial, swap(sent, "core"), routes)
    got = lax.all_to_all(packed, ("xh", "y"), split_axis=0, concat_axis=0, tiled=True).astype(F32)
    outputs = jnp.sum(got[:, :tok], axis=0).astype(BF)
    extra = jnp.sum(got[:, tok : tok + segs], axis=0)
    merge_grad = sum(extra[:, 128 * i : 128 * i + experts] for i in range(3))
    copies = jnp.broadcast_to(merge_grad[None], (n_seq, segs, experts))
    merge_grad = jnp.sum(lax.all_to_all(copies, SEQ, split_axis=0, concat_axis=0, tiled=True), axis=0)
    grad_route = route_gradient(merge_grad, keep)
    return outputs[:, :width], outputs[:, width:], grad_route


def solution(mesh):
    split = Mesh(mesh.devices.reshape(NZ, 2, 2, 4, 2), SEQ + COL)
    return jax.shard_map(
        on_device,
        mesh=split,
        in_specs=(
            P(SEQ, None),
            P(None, SEQ, COL),
            P(None, SEQ, COL),
            P(None, COL, SEQ),
            P(None, SEQ),
            P(),
            P(),
        ),
        out_specs=(P(COL, SEQ), P(COL, SEQ), P()),
        check_vma=False,
    )
```

```python
import jax
import jax.numpy as jnp
from jax import lax
from jax.experimental import pallas as pl
from jax.experimental.pallas import tpu as pltpu
from jax.sharding import Mesh, PartitionSpec as P

SEQ = ("z", "xl")
COL = ("xh", "y", "core")
NZ = 8
TILE = 32
ROWS = 128
EXTRA = 16
BF = jnp.bfloat16
F32 = jnp.float32


def routing(route, doc_start):
    own = route.astype(F32) / 1024.0
    prev = jnp.concatenate([own[:1], own[:-1]], axis=0)
    first = jnp.arange(route.shape[0]) == 0
    keep = jnp.logical_or(first, doc_start == 1)
    return jnp.where(keep[:, None], own, prev), keep


def route_gradient(merge_grad, keep):
    own_part = jnp.where(keep[:, None], merge_grad, jnp.float32(0.0))
    next_part = jnp.where(keep[:, None], jnp.float32(0.0), merge_grad)
    next_part = jnp.concatenate([next_part[1:], jnp.zeros_like(next_part[:1])], axis=0)
    return (own_part + next_part) / 1024.0


def dot(a, b, ca, cb):
    return lax.dot_general(a, b, (((ca,), (cb,)), ((), ())), preferred_element_type=F32)


def params(mib):
    return pltpu.CompilerParams(vmem_limit_bytes=mib * 1024 * 1024)


def cost(flops, nbytes):
    return pl.CostEstimate(flops=flops, bytes_accessed=nbytes, transcendentals=0)


def by_width(rows, width):
    n = rows.shape[1] // width

    def kernel(rows_r, out):
        for i in range(n):
            out[i] = rows_r[:, i * width : (i + 1) * width]

    return pl.pallas_call(
        kernel,
        out_shape=jax.ShapeDtypeStruct((n, rows.shape[0], width), rows.dtype),
        compiler_params=params(8),
        cost_estimate=cost(0, 4 * rows.size),
        name="by_width",
    )(rows)


def merge_kernel(n, *refs):
    table = refs[0][...]
    experts, rows, width = refs[1].shape
    for w, out in zip(refs[1 : 1 + n], refs[1 + n :]):
        for j in range(0, rows, TILE):
            tile = w[:, j : j + TILE, :].reshape(experts * TILE, width)
            out[:, j : j + TILE, :] = dot(table, tile, 1, 0).astype(BF).reshape(experts, TILE, width)


def merge(table, *weights):
    n = len(weights)
    experts, rows, width = weights[0].shape
    size = weights[0].size
    block = pl.BlockSpec((experts, ROWS, width), lambda i: (0, i, 0))
    return pl.pallas_call(
        lambda *refs: merge_kernel(n, *refs),
        grid=(pl.cdiv(rows, ROWS),),
        in_specs=[pl.BlockSpec(table.shape, lambda i: (0, 0))] + [block] * n,
        out_specs=[block] * n,
        out_shape=[pltpu.HBM(w.shape, BF) for w in weights],
        compiler_params=params(14),
        cost_estimate=cost(2 * 256 * n * size, 4 * n * size),
        name="merge",
    )(table, *weights)


def at_segment(k):
    return lambda i, s: (lax.rem(s[0] + k, NZ), 0, 0)


def at_own(k):
    return lambda i, s: (2 * lax.rem(s[0] + k, NZ) + s[1], 0, 0)


def at_other(k):
    return lambda i, s: (2 * lax.rem(s[0] + k, NZ) + 1 - s[1], 0, 0)


def whole(shape):
    return pl.BlockSpec(shape, lambda i, s: (0,) * len(shape))


def partial_products(where, groups, mats, blocks, front, after=()):
    groups = [g if isinstance(g, tuple) else (g,) for g in groups]
    ks = [k for g in groups for k in g]
    place = [(g, i) for g, ks_of in enumerate(groups) for i in range(len(ks_of))]
    rows, width = mats[0].shape[1:]
    tok = blocks.shape[1]
    n = len(mats)
    per = n + 2
    back = n * rows - front
    specs = []
    args = []
    for k in ks:
        specs += [pl.BlockSpec((1, rows, width), at_segment(k))] * n
        specs += [pl.BlockSpec((1, tok, width), at_own(k)), pl.BlockSpec((1, tok, width), at_other(k))]
        args += list(mats) + [blocks, blocks]
    specs += [pl.BlockSpec(memory_space=pl.ANY)] * len(after)
    shapes = []
    if front:
        shapes = [jax.ShapeDtypeStruct((len(g), front, tok), BF) for g in groups]
        shapes += [jax.ShapeDtypeStruct((front, tok), F32)] * len(ks)
    if back:
        shapes += [jax.ShapeDtypeStruct((back, 2 * tok), F32)] * len(ks)

    def kernel(s_ref, *refs):
        outs = refs[per * len(ks) + len(after) :]
        for i in range(len(ks)):
            part = refs[per * i : per * (i + 1)]
            both = jnp.concatenate([part[n][0], part[n + 1][0]], axis=0)
            for m in range(n):
                r = dot(part[m][0], both, 1, 1)
                at = m * rows
                cut = min(max(front - at, 0), rows)
                if cut:
                    outs[place[i][0]][place[i][1], at : at + cut, :] = r[:cut, tok:].astype(BF)
                    outs[len(groups) + i][at : at + cut, :] = r[:cut, :tok]
                if cut < rows:
                    outs[len(shapes) - len(ks) + i][at + cut - front : at + rows - front, :] = r[cut:, :]

    found = pl.pallas_call(
        kernel,
        grid_spec=pltpu.PrefetchScalarGridSpec(
            num_scalar_prefetch=1,
            grid=(1,),
            in_specs=specs,
            out_specs=[whole(s.shape) for s in shapes],
        ),
        out_shape=shapes,
        compiler_params=params(24),
        cost_estimate=cost(4 * len(ks) * n * rows * width * tok, 8 * len(ks) * n * rows * width),
        name="products",
    )(where, *args, *after)
    g = len(groups) if front else 0
    n = len(ks) if front else 0
    return found[:g], dict(zip(ks, found[g : g + n])), dict(zip(ks, found[g + n :]))


def diagonal(n):
    return lax.broadcasted_iota(jnp.int32, (n, 128), 0) == lax.broadcasted_iota(jnp.int32, (n, 128), 1)


def in_terms(x):
    terms = []
    for _ in range(3):
        terms.append(x.astype(BF).astype(F32))
        x = x - terms[-1]
    return terms + [jnp.zeros_like(x)]


def pack(keep, came, routes):
    segs, tok, width = keep.shape

    def kernel(keep_r, came_r, routes_r, out):
        at = lax.broadcasted_iota(jnp.int32, (segs, 128), 0)
        table = jnp.zeros((segs, 128), F32)
        for d in range(segs):
            out[d, :tok, :] = (keep_r[d] + came_r[d, :tok, :].astype(F32)).astype(BF)
            tail = came_r[d, tok:, :].astype(F32)
            row = routes_r[d, :1, :] + (tail[:1, :128] + tail[:1, 128:256] + tail[:1, 256:384])
            table = jnp.where(at == d, row, table)
        extra = jnp.concatenate(in_terms(table), axis=1)
        extra = jnp.concatenate([extra, jnp.zeros_like(extra)], axis=0).astype(BF)
        for d in range(segs):
            out[d, tok:, :] = extra

    return pl.pallas_call(
        kernel,
        out_shape=jax.ShapeDtypeStruct(came.shape, BF),
        compiler_params=params(14),
        cost_estimate=cost(2 * keep.size, 8 * keep.size),
        name="pack",
    )(keep, came, routes)


def segment_backward(where, k, act, own, other, tok_blocks, cot_blocks, merged, weights, so_far):
    segs, rows, width = merged[0].shape
    tok = tok_blocks.shape[1]

    def kernel(s_ref, act_r, own_r, oth_r, to_r, tp_r, co_r, cp_r, g_r, u_r, d_r, wg_r, wu_r, wd_r, *rest):
        keep, send, route, o_gate, o_up, o_down = rest[-6:]
        a = act_r[...]
        gg = jnp.concatenate([own_r[:rows, :], oth_r[:rows, :]], axis=1)
        gu = jnp.concatenate([own_r[rows:, :], oth_r[rows:, :]], axis=1)
        tokens = jnp.concatenate([to_r[0], tp_r[0]], axis=0)
        cots = jnp.concatenate([co_r[0], cp_r[0]], axis=0)
        o_gate[...] = dot(gg, tokens, 1, 0).astype(BF)
        o_up[...] = dot(gu, tokens, 1, 0).astype(BF)
        o_down[...] = dot(a, cots, 1, 0).astype(BF)
        result = jnp.concatenate([dot(a, d_r[0], 0, 0), dot(gg, g_r[0], 0, 0) + dot(gu, u_r[0], 0, 0)], axis=1)

        @pl.when(s_ref[2] == 0)
        def _():
            keep[0] = result[:tok]
            send[0, :tok, :] = result[tok:].astype(BF)

        @pl.when(s_ref[2] == 1)
        def _():
            keep[0] = result[tok:]
            send[0, :tok, :] = result[:tok].astype(BF)

        def part(at, total):
            p = o_gate[at, :].astype(F32) * wg_r[:, at, :].astype(F32)
            p += o_up[at, :].astype(F32) * wu_r[:, at, :].astype(F32)
            p += o_down[at, :].astype(F32) * wd_r[:, at, :].astype(F32)
            return total + (p[:, :8, :] + p[:, 8:, :])

        def step(j, total):
            for i in range(4):
                total = part(pl.ds(pl.multiple_of(j * 64 + i * 16, 16), 16), total)
            return total

        total = lax.fori_loop(0, rows // 64, step, jnp.zeros((segs, 8, width), F32))
        for at in range(rows // 64 * 64, rows, 16):
            total = part(pl.ds(at, 16), total)
        sums = jnp.sum(jnp.sum(total, axis=1), axis=1, keepdims=True)
        row = jnp.sum(jnp.where(diagonal(segs), sums, 0.0), axis=0, keepdims=True)
        route[0] = jnp.broadcast_to(row, (8, 128))
        send[0, tok:, :] = jnp.broadcast_to(jnp.concatenate(in_terms(row), axis=1), (EXTRA, 4 * 128)).astype(BF)

    shapes = [
        jax.ShapeDtypeStruct((segs, tok, 2 * width), F32),
        jax.ShapeDtypeStruct((segs, tok + EXTRA, 2 * width), BF),
        jax.ShapeDtypeStruct((segs, 8, 128), F32),
    ]
    seg = pl.BlockSpec((1, rows, width), at_segment(k))
    specs = [
        whole(act.shape),
        whole(own.shape),
        whole(other.shape),
        pl.BlockSpec((1, tok, width), at_own(k)),
        pl.BlockSpec((1, tok, width), at_other(k)),
        pl.BlockSpec((1, tok, width), at_own(k)),
        pl.BlockSpec((1, tok, width), at_other(k)),
        seg,
        seg,
        seg,
    ]
    specs += [pl.BlockSpec(memory_space=pltpu.VMEM)] * 3
    args = [act, own, other, tok_blocks, tok_blocks, cot_blocks, cot_blocks, *merged, *weights]
    aliases = {}
    if so_far is not None:
        aliases = {1 + len(args) + i: i for i in range(3)}
        specs += [pl.BlockSpec(memory_space=pl.ANY)] * 3
        args += list(so_far)
    return pl.pallas_call(
        kernel,
        grid_spec=pltpu.PrefetchScalarGridSpec(
            num_scalar_prefetch=1,
            grid=(1,),
            in_specs=specs,
            out_specs=[pl.BlockSpec((1,) + x.shape[1:], at_segment(k)) for x in shapes],
            scratch_shapes=[pltpu.VMEM((rows, width), BF)] * 3,
        ),
        out_shape=shapes,
        input_output_aliases=aliases,
        compiler_params=params(14),
        cost_estimate=cost(24 * rows * width * tok, 20 * rows * width),
        name="backward",
    )(where, *args)


def shift(x, axis, n, by):
    return lax.ppermute(x, axis, [(i, (i + by) % n) for i in range(n)])


def swap(x, axis):
    return shift(x, axis, 2, 1)


def add(a, b):
    return a.astype(F32) + b.astype(F32)


def middle(rows):
    return rows // 2 // 16 * 16


def both_ways(up, down):
    return shift(up, "z", NZ, 1), shift(down, "z", NZ, -1)


def ring_sum(blocks):
    half = middle(blocks[4].shape[0])
    up, down = both_ways(blocks[4][:half].astype(BF), blocks[4][half:].astype(BF))
    up = jnp.concatenate([add(up, blocks[3][:half]), blocks[3][half:]], axis=0).astype(BF)
    down = jnp.concatenate([blocks[5][:half], add(down, blocks[5][half:])], axis=0).astype(BF)
    up, down = both_ways(up, down)
    up, down = both_ways(add(up, blocks[2]).astype(BF), add(down, blocks[6]).astype(BF))
    up, down = both_ways(add(up, blocks[1]).astype(BF), add(down, blocks[7]).astype(BF))
    return add(up, down) + blocks[0]


def farthest(up, down):
    half = middle(up.shape[0])
    return jnp.concatenate(both_ways(up[:half], down[half:]), axis=0)


def on_device(tokens, gate_weight, up_weight, down_weight, cotangent, route, doc_start):
    tok, width_all = tokens.shape
    experts, width, cols = gate_weight.shape
    segs = route.shape[0]
    n_seq = 2 * NZ
    z, xl, core = (lax.axis_index(a).astype(jnp.int32) for a in ("z", "xl", "core"))
    where = jnp.stack([z, xl, (xl + core) % 2])
    used, keep = routing(route, doc_start)
    table = used.astype(BF)[:, None, :, None] * jnp.eye(TILE, dtype=BF)[None, :, None, :]
    table = table.reshape(segs * TILE, experts * TILE)

    tok_blocks = lax.all_to_all(by_width(tokens, width), SEQ, split_axis=0, concat_axis=0, tiled=True)
    cot_blocks = cotangent.reshape(n_seq, tok, width)
    gate_weight = gate_weight.swapaxes(1, 2)
    up_weight = up_weight.swapaxes(1, 2)

    (m_down,) = merge(table, down_weight)
    m_gate, m_up = merge(table, gate_weight, up_weight)

    order = (4, 3, 5, 2, 6, 1, 7, 0)
    _, _, acting = partial_products(where, order, (m_down,), cot_blocks, 0)
    both = ring_sum(acting)
    grad_act = both[:, :tok] + swap(both[:, tok:].astype(BF), "xl").astype(F32)

    first, later = ((4, 3, 5),), ((2, 6), (1, 7), (0,))
    mats = (m_gate, m_up)
    sends, kept, _ = partial_products(where, first, mats, tok_blocks, 2 * cols, after=(acting[4],))
    came = [swap(sends[0], "xl")]
    sends, more, _ = partial_products(where, later, mats, tok_blocks, 2 * cols, after=(acting[4],))
    came[0], *sends = lax.optimization_barrier((came[0], *sends))
    came += [swap(block, "xl") for block in sends]
    kept.update(more)
    parts = {}
    for ks, block in zip(first + later, came):
        for i, k in enumerate(ks):
            parts[k] = add(kept[k], block[i])
    pre = ring_sum(parts)

    gate, up = pre[:cols], pre[cols:]
    sig = jax.nn.sigmoid(gate)
    act = (gate * sig * up).astype(BF)
    grad_gate = grad_act * up * sig * (1.0 + gate * (1.0 - sig))
    grad_up = grad_act * gate * sig
    grads = jnp.concatenate([grad_gate, grad_up], axis=0).astype(BF)

    act_and_grads = jnp.concatenate([act, grads], axis=0)
    came = swap(act_and_grads, "xl")
    other = {0: came[cols:]}
    own, acts = {0: grads}, {0: jnp.concatenate([act, came[:cols]], axis=1)}
    sums = None

    def swap_pair(*ks):
        pair = swap(jnp.stack([own[k] for k in ks]), "xl")
        other.update({k: pair[i] for i, k in enumerate(ks)})

    def backward(*ks):
        found = sums
        for k in ks:
            found = segment_backward(
                where,
                k,
                acts[k],
                own[k],
                other[k],
                tok_blocks,
                cot_blocks,
                (m_gate, m_up, m_down),
                (gate_weight, up_weight, down_weight),
                found,
            )
        return found

    own[7], own[1] = both_ways(grads, grads)
    swap_pair(7, 1)
    first_act, _ = lax.optimization_barrier((acts[0], own[7]))
    acts[7], acts[1] = both_ways(first_act, first_act)
    own[6], own[2] = both_ways(own[7], own[1])
    swap_pair(6, 2)
    sums = backward(0, 7, 1)
    up, down = both_ways(own[6], own[2])
    own[5], own[3], _ = lax.optimization_barrier((up, down, sums[2]))
    swap_pair(5, 3)
    own[4] = farthest(own[5], own[3])
    swap_pair(4)
    acts[6], acts[2] = both_ways(acts[7], acts[1])
    acts[5], acts[3] = both_ways(acts[6], acts[2])
    acts[4] = farthest(acts[5], acts[3])
    sums = backward(6, 2, 5, 3, 4)
    partial, sent, routes = sums
    packed = pack(partial, swap(sent, "core"), routes)
    got = lax.all_to_all(packed, ("xh", "y"), split_axis=0, concat_axis=0, tiled=True).astype(F32)
    outputs = jnp.sum(got[:, :tok], axis=0).astype(BF)
    extra = jnp.sum(got[:, tok : tok + segs], axis=0)
    merge_grad = sum(extra[:, 128 * i : 128 * i + experts] for i in range(3))
    copies = jnp.broadcast_to(merge_grad[None], (n_seq, segs, experts))
    merge_grad = jnp.sum(lax.all_to_all(copies, SEQ, split_axis=0, concat_axis=0, tiled=True), axis=0)
    grad_route = route_gradient(merge_grad, keep)
    return outputs[:, :width], outputs[:, width:], grad_route


def solution(mesh):
    split = Mesh(mesh.devices.reshape(NZ, 2, 2, 4, 2), SEQ + COL)
    return jax.shard_map(
        on_device,
        mesh=split,
        in_specs=(
            P(SEQ, None),
            P(None, SEQ, COL),
            P(None, SEQ, COL),
            P(None, COL, SEQ),
            P(None, SEQ),
            P(),
            P(),
        ),
        out_specs=(P(COL, SEQ), P(COL, SEQ), P()),
        check_vma=False,
    )
```
